32 devices in a mesh: pipe: 8 (over z, y), tensor: 4 (over x, core).
Axes of the slice: x: 2, y: 2, z: 4, core: 2. Of those that a mesh axis runs over, the one named last changes fastest.
Arguments:
- residual: bfloat16 [8, 128, 4096], P('pipe'), may hold values from -4 to 4
- out_proj: bfloat16 [8, 4096, 4096], P('pipe', 'tensor'), may hold values from -0.25 to 0.25
- attn_in: bfloat16 [8, 3, 128, 4096], P('pipe', None, None, 'tensor'), may hold values from -9 to 9
- stash_slots: bfloat16 [8, 2, 3, 128, 4096], P('pipe', None, None, None, 'tensor'), may hold values from -9 to 9
- grad_in: bfloat16 [8, 128, 4096], P('pipe'), may hold values from -6 to 6
- stash_slot: int32 [8], replicated, may hold values from 0 to 1
Outputs:
- fwd_out: bfloat16 [8, 128, 4096], P('pipe')
- qkv_grad: bfloat16 [8, 3, 128, 4096], P('pipe', None, None, 'tensor')
- evicted: bfloat16 [8, 3, 128, 4096], P('pipe', None, None, 'tensor')
The draws below stay inside these ranges and needn't reach their ends.
All inputs are finite; a program needn't handle non-finite values.
Results may differ from the reference program's by a relative error of at most 0.0065.
Values may be sent and summed in bfloat16 or wider, within the bound.
A program may use at most 64 MiB of HBM per device.

```python
import jax
import jax.numpy as jnp
from jax import lax

D = 4096
HD = 128
HEADS = 32
ROWS = 128
SLOTS = 2
SECTIONS = 8


def attention_law(key, leading):
    full_shape = leading + (3, ROWS, HEADS * HD)
    return jnp.clip(jax.random.normal(key, full_shape, jnp.float32), -6.0, 6.0)


def draw_attn_in(key, part):
    return attention_law(jax.random.fold_in(key, 1), (SECTIONS,)).astype(jnp.bfloat16)


def draw_stash_slots(key, part):
    return attention_law(jax.random.fold_in(key, 2), (SECTIONS, SLOTS)).astype(jnp.bfloat16)


def touch_ends(values, own_key, smallest, largest):
    spot = [jax.random.randint(jax.random.fold_in(own_key, axis), (), 0, length) for axis, length in enumerate(values.shape)]
    longest = values.shape.index(max(values.shape))
    next_to = spot[:longest] + [(spot[longest] + 1) % values.shape[longest]] + spot[longest + 1:]
    return values.at[tuple(spot)].set(smallest).at[tuple(next_to)].set(largest)


def shard_levels(key, shape, pieces, smallest, top_value):
    level = 1.0
    for position, parts in pieces:
        steps = jax.random.uniform(jax.random.fold_in(jax.random.fold_in(key, 6), position), (parts,), jnp.float32, smallest / len(pieces), top_value / len(pieces))
        level = level * jnp.repeat(jnp.exp(steps), shape[position] // parts).reshape((-1,) + (1,) * (len(shape) - 1 - position))
    return level


def normal_values(key, extent, deviation, bound, pieces=(), kind=jnp.bfloat16):
    result = jax.random.normal(key, extent, jnp.float32) * deviation
    if len(pieces) > 0:
        result = shard_levels(key, extent, pieces, -0.22, 0.18) * result
    return jnp.clip(result, min=-bound, max=bound).astype(kind)


def setup_inputs(seed: int = 0) -> dict:
    streams_of = jax.random.split(jax.random.key(seed), 7)
    residual = normal_values(streams_of[0], (SECTIONS, ROWS, D), 0.3, 4.0, ((0, 8),))
    out_proj = normal_values(streams_of[1], (SECTIONS, HEADS * HD, D), (HEADS * HD // 8) ** -0.5, 0.25, ((0, 8), (1, 4)))
    attn_in = draw_attn_in(jax.random.fold_in(streams_of[6], 71), 0)
    stash_slots = draw_stash_slots(jax.random.fold_in(streams_of[6], 71), 0)
    grad_in = normal_values(streams_of[4], (SECTIONS, ROWS, D), 1.0, 6.0, ((0, 8),))
    stash_slot = touch_ends(jax.random.randint(streams_of[5], (SECTIONS,), 0, SLOTS), jax.random.fold_in(streams_of[5], 1), 0, SLOTS - 1).astype(jnp.int32)
    return dict(residual=residual, out_proj=out_proj, attn_in=attn_in, stash_slots=stash_slots, grad_in=grad_in, stash_slot=stash_slot)


def head_probs(query_in, key_in):
    length = query_in.shape[0]
    query_heads = query_in.astype(jnp.float32).reshape(length, -1, HD)
    key_heads = key_in.astype(jnp.float32).reshape(length, -1, HD)
    scores = jnp.einsum("ihd,jhd->hij", query_heads, key_heads) * (HD ** -0.5)
    row_ids = jnp.arange(length, dtype=jnp.int32)
    allowed = row_ids[:, None] >= row_ids[None, :]
    scores = jnp.where(allowed[None], scores, -jnp.inf)
    return jax.nn.softmax(scores, axis=-1)


def attend(inputs):
    length = inputs.shape[1]
    attn_probs = head_probs(inputs[0], inputs[1])
    probs_low = lax.optimization_barrier(attn_probs.astype(jnp.bfloat16)).astype(jnp.float32)
    value_heads = inputs[2].astype(jnp.float32).reshape(length, -1, HD)
    context = jnp.einsum("hij,jhd->ihd", probs_low, value_heads)
    return context.reshape(length, -1).astype(jnp.bfloat16)


def attend_back(stored, grad_context):
    length = stored.shape[1]
    scale_factor = HD ** -0.5
    attn_probs = head_probs(stored[0], stored[1])
    grad_heads = lax.optimization_barrier(grad_context).astype(jnp.float32).reshape(length, -1, HD)
    query_heads = stored[0].astype(jnp.float32).reshape(length, -1, HD)
    key_heads = stored[1].astype(jnp.float32).reshape(length, -1, HD)
    value_heads = stored[2].astype(jnp.float32).reshape(length, -1, HD)
    grad_probs = jnp.einsum("ihd,jhd->hij", grad_heads, value_heads)
    row_delta = jnp.sum(attn_probs * grad_probs, axis=-1, keepdims=True)
    grad_scores = (attn_probs * (grad_probs - row_delta)).astype(jnp.bfloat16)
    grad_scores = lax.optimization_barrier(grad_scores).astype(jnp.float32)
    probs_low = lax.optimization_barrier(attn_probs.astype(jnp.bfloat16)).astype(jnp.float32)
    grad_query = jnp.einsum("hij,jhd->ihd", grad_scores, key_heads) * scale_factor
    grad_key = jnp.einsum("hij,ihd->jhd", grad_scores, query_heads) * scale_factor
    grad_value = jnp.einsum("hij,ihd->jhd", probs_low, grad_heads)
    stacked = jnp.stack([grad_query, grad_key, grad_value], axis=0)
    return stacked.reshape(3, length, -1).astype(jnp.bfloat16)


def forward_section(inputs, resid_rows, weight):
    context = attend(inputs)
    branch = jnp.dot(context, weight, preferred_element_type=jnp.float32)
    return (resid_rows.astype(jnp.float32) + branch).astype(jnp.bfloat16)


def backward_section(stored, grad_rows, weight):
    grad_context = lax.dot_general(grad_rows, weight, (((1,), (1,)), ((), ())), preferred_element_type=jnp.float32)
    return attend_back(stored, grad_context.astype(jnp.bfloat16))


def reference(residual, out_proj, attn_in, stash_slots, grad_in, stash_slot):
    section_ids = jnp.arange(SECTIONS, dtype=jnp.int32)
    partner = ((section_ids + SECTIONS // 2) % SECTIONS).astype(jnp.int32)
    section_outs = lax.map(lambda items: forward_section(items[0], items[1], items[2]), (attn_in, residual, out_proj))
    fwd_out = jnp.roll(section_outs, 1, axis=0)
    stored = stash_slots[partner, stash_slot]
    all_grads = lax.map(lambda items: backward_section(items[0], items[1], items[2]), (stored, grad_in, out_proj))
    evicted = attn_in[partner]
    return fwd_out, all_grads, evicted
```

```python
import functools

import jax
import jax.numpy as jnp
from jax import lax
from jax.experimental import pallas as pl
from jax.experimental.pallas import tpu as pltpu
from jax.sharding import PartitionSpec as P

HD = 128
MESH = pl.DeviceIdType.MESH
VMEM_LIMIT = 40 * 1024 * 1024
ACROSS = (((1,), (1,)), ((), ()))
DOWN = (((0,), (0,)), ((), ()))


def mult(a, b, dims):
    return lax.dot_general(a, b, dims, preferred_element_type=jnp.float32)


def head_probs(query, key):
    length = query.shape[0]
    scores = mult(query, key, ACROSS) * HD ** (-0.5)
    row_ids = lax.broadcasted_iota(jnp.int32, (length, length), 0)
    col_ids = lax.broadcasted_iota(jnp.int32, (length, length), 1)
    scores = jnp.where(row_ids >= col_ids, scores, -jnp.inf)
    top = jnp.max(scores, axis=-1, keepdims=True)
    raised = jnp.exp(scores - top)
    return raised / jnp.sum(raised, axis=-1, keepdims=True)


def tick(
    sections,
    group,
    slot_ref,
    residual_ref,
    weight_ref,
    attn_ref,
    stash_ref,
    grad_ref,
    fwd_ref,
    qkv_ref,
    evict_ref,
    weight,
    attn,
    stash,
    grad,
    resid,
    request,
    stored,
    context,
    grad_context,
    own_sum,
    sums_out,
    sums_in,
    piece_out,
    piece_in,
    qkv,
    local_sem,
    evict_send,
    evict_recv,
    request_send,
    request_recv,
    sums_send,
    sums_recv,
    piece_send,
    piece_recv,
    gather_send,
    gather_recv,
):
    section = lax.axis_index("pipe")
    shard = lax.axis_index("tensor")
    partner = lax.rem(section + sections // 2, sections)
    following = lax.rem(section + 1, sections)
    before = lax.rem(section + sections - 1, sections)
    parts, rows, local = attn.shape
    width = piece_out.shape[1]
    heads = local // HD

    def peer(distance):
        return lax.rem(shard + distance, group)

    def lanes(index, size):
        return pl.ds(pl.multiple_of(index * size, size), size)

    loads = []
    for number, (source, target) in enumerate(
        (
            (stash_ref.at[0], stash),
            (attn_ref.at[0], attn),
            (weight_ref.at[0], weight),
            (grad_ref.at[0], grad),
            (residual_ref.at[0, :, lanes(shard, width)], resid),
        )
    ):
        load = pltpu.make_async_copy(source, target, local_sem.at[number])
        load.start()
        loads.append(load)

    barrier = pltpu.get_barrier_semaphore()
    for other in (partner, following, before):
        pl.semaphore_signal(barrier, inc=1, device_id=(other, shard), device_id_type=MESH)
    for distance in range(1, group):
        pl.semaphore_signal(
            barrier, inc=1, device_id=(section, peer(distance)), device_id_type=MESH
        )
    pl.semaphore_wait(barrier, 3 + group - 1)

    evictions = [
        pltpu.make_async_remote_copy(
            src_ref=attn_ref.at[0, part],
            dst_ref=evict_ref.at[0, part],
            send_sem=evict_send.at[part],
            recv_sem=evict_recv.at[part],
            device_id=(partner, shard),
            device_id_type=MESH,
        )
        for part in range(parts)
    ]
    requests = [
        pltpu.make_async_remote_copy(
            src_ref=request.at[part],
            dst_ref=stored.at[part],
            send_sem=request_send.at[part],
            recv_sem=request_recv.at[part],
            device_id=(partner, shard),
            device_id_type=MESH,
        )
        for part in range(parts)
    ]

    evictions[0].start()
    wanted = slot_ref[partner]
    loads[0].wait()
    for part in range(parts):
        request[part] = stash[wanted, part]
        requests[part].start()

    loads[1].wait()

    def attend(head, _):
        cols = lanes(head, HD)
        probs = head_probs(attn[0, :, cols], attn[1, :, cols]).astype(jnp.bfloat16)
        values = attn[2, :, cols]
        context[:, cols] = jnp.dot(
            probs, values, preferred_element_type=jnp.float32
        ).astype(jnp.bfloat16)
        return 0

    lax.fori_loop(0, heads, attend, 0, unroll=2)

    loads[2].wait()
    transfers = []
    for distance in range(1, group):
        target = peer(distance)
        sums_out[distance - 1] = jnp.dot(
            context[...], weight[:, lanes(target, width)], preferred_element_type=jnp.float32
        )
        transfer = pltpu.make_async_remote_copy(
            src_ref=sums_out.at[distance - 1],
            dst_ref=sums_in.at[distance - 1],
            send_sem=sums_send.at[distance - 1],
            recv_sem=sums_recv.at[distance - 1],
            device_id=(section, target),
            device_id_type=MESH,
        )
        transfer.start()
        transfers.append(transfer)
    loads[4].wait()
    own_sum[...] = resid[...].astype(jnp.float32) + jnp.dot(
        context[...], weight[:, lanes(shard, width)], preferred_element_type=jnp.float32
    )

    loads[3].wait()
    tile = min(local, 2 * HD)

    def back_project(step, _):
        cols = lanes(step, tile)
        grad_context[:, cols] = mult(grad[...], weight[cols, :], ACROSS).astype(jnp.bfloat16)
        return 0

    lax.fori_loop(0, local // tile, back_project, 0)

    for transfer in transfers:
        transfer.wait()
    total = own_sum[...]
    for distance in range(1, group):
        total = total + sums_in[distance - 1]
    piece_out[...] = total.astype(jnp.bfloat16)
    hand_over = pltpu.make_async_remote_copy(
        src_ref=piece_out,
        dst_ref=piece_in,
        send_sem=piece_send.at[0],
        recv_sem=piece_recv.at[0],
        device_id=(following, shard),
        device_id_type=MESH,
    )
    hand_over.start()
    for part in range(1, parts):
        evictions[part].start()

    hand_over.wait()
    own_columns = lanes(shard, width)
    gathers = []
    for distance in range(1, group):
        gather = pltpu.make_async_remote_copy(
            src_ref=piece_in,
            dst_ref=fwd_ref.at[0, :, own_columns],
            send_sem=gather_send.at[distance - 1],
            recv_sem=gather_recv.at[distance - 1],
            device_id=(section, peer(distance)),
            device_id_type=MESH,
        )
        gather.start()
        gathers.append(gather)
    keep = pltpu.make_async_copy(piece_in, fwd_ref.at[0, :, own_columns], local_sem.at[5])
    keep.start()

    for copy in requests:
        copy.wait()

    def attend_back(head, _):
        cols = lanes(head, HD)
        query, key, value = (stored[part, :, cols] for part in range(3))
        grads = grad_context[:, cols]
        probs = head_probs(query, key)
        grad_probs = mult(grads, value, ACROSS)
        row_delta = jnp.sum(probs * grad_probs, axis=-1, keepdims=True)
        grad_scores = (probs * (grad_probs - row_delta)).astype(jnp.bfloat16)
        probs_low = probs.astype(jnp.bfloat16)
        grad_query = jnp.dot(grad_scores, key, preferred_element_type=jnp.float32)
        grad_key = mult(grad_scores, query, DOWN)
        qkv[0, :, cols] = (grad_query * HD ** (-0.5)).astype(jnp.bfloat16)
        qkv[1, :, cols] = (grad_key * HD ** (-0.5)).astype(jnp.bfloat16)
        qkv[2, :, cols] = mult(probs_low, grads, DOWN).astype(jnp.bfloat16)
        return 0

    lax.fori_loop(0, heads, attend_back, 0, unroll=2)
    put = pltpu.make_async_copy(qkv, qkv_ref.at[0], local_sem.at[6])
    put.start()

    keep.wait()
    put.wait()
    for copy in gathers:
        copy.wait()
    for copy in evictions:
        copy.wait()


def settle(*refs):
    count = (len(refs) - 1) // 2
    sources, targets, sem = refs[:count], refs[count : 2 * count], refs[-1]
    copies = []
    for number, (source, target) in enumerate(zip(sources, targets)):
        copy = pltpu.make_async_copy(source, target, sem.at[number])
        copy.start()
        copies.append(copy)
    for copy in copies:
        copy.wait()


def on_device(residual, out_proj, attn_in, stash_slots, grad_in, stash_slot):
    sections = lax.axis_size("pipe")
    group = lax.axis_size("tensor")
    _, parts, rows, local = attn_in.shape
    slots = stash_slots.shape[1]
    depth = residual.shape[2]
    width = depth // group
    anywhere = pl.BlockSpec(memory_space=pl.ANY)
    results = (
        jax.ShapeDtypeStruct((1, rows, depth), jnp.bfloat16),
        jax.ShapeDtypeStruct((1, parts, rows, local), jnp.bfloat16),
        jax.ShapeDtypeStruct((1, parts, rows, local), jnp.bfloat16),
    )
    low, full = jnp.bfloat16, jnp.float32
    flops = 4 * rows * local * depth + 16 * rows * rows * local
    made = pl.pallas_call(
        functools.partial(tick, sections, group),
        out_shape=results,
        in_specs=[pl.BlockSpec(memory_space=pltpu.SMEM)] + [anywhere] * 5,
        out_specs=(anywhere,) * 3,
        scratch_shapes=[
            pltpu.VMEM((local, depth), low),
            pltpu.VMEM((parts, rows, local), low),
            pltpu.VMEM((slots, parts, rows, local), low),
            pltpu.VMEM((rows, depth), low),
            pltpu.VMEM((rows, width), low),
            pltpu.VMEM((parts, rows, local), low),
            pltpu.VMEM((parts, rows, local), low),
            pltpu.VMEM((rows, local), low),
            pltpu.VMEM((rows, local), low),
            pltpu.VMEM((rows, width), full),
            pltpu.VMEM((group - 1, rows, width), full),
            pltpu.VMEM((group - 1, rows, width), full),
            pltpu.VMEM((rows, width), low),
            pltpu.VMEM((rows, width), low),
            pltpu.VMEM((parts, rows, local), low),
            pltpu.SemaphoreType.DMA((7,)),
            pltpu.SemaphoreType.DMA((parts,)),
            pltpu.SemaphoreType.DMA((parts,)),
            pltpu.SemaphoreType.DMA((parts,)),
            pltpu.SemaphoreType.DMA((parts,)),
            pltpu.SemaphoreType.DMA((group - 1,)),
            pltpu.SemaphoreType.DMA((group - 1,)),
            pltpu.SemaphoreType.DMA((1,)),
            pltpu.SemaphoreType.DMA((1,)),
            pltpu.SemaphoreType.DMA((group - 1,)),
            pltpu.SemaphoreType.DMA((group - 1,)),
        ],
        compiler_params=pltpu.CompilerParams(
            collective_id=0, has_side_effects=True, vmem_limit_bytes=VMEM_LIMIT
        ),
        cost_estimate=pl.CostEstimate(
            flops=flops, bytes_accessed=2 * local * depth, transcendentals=2 * rows * local
        ),
        name="tick",
    )(stash_slot, residual, out_proj, attn_in, stash_slots, grad_in)
    return pl.pallas_call(
        settle,
        out_shape=results,
        in_specs=[anywhere] * 3,
        out_specs=(anywhere,) * 3,
        scratch_shapes=[pltpu.SemaphoreType.DMA((3,))],
        name="settle",
    )(*made)


def solution(mesh):
    in_specs = (
        P("pipe", None, None),
        P("pipe", "tensor", None),
        P("pipe", None, None, "tensor"),
        P("pipe", None, None, None, "tensor"),
        P("pipe", None, None),
        P(),
    )
    out_specs = (
        P("pipe", None, None),
        P("pipe", None, None, "tensor"),
        P("pipe", None, None, "tensor"),
    )
    return jax.shard_map(
        on_device, mesh=mesh, in_specs=in_specs, out_specs=out_specs, check_vma=False
    )
```

```python
import functools

import jax
import jax.numpy as jnp
from jax import lax
from jax.experimental import pallas as pl
from jax.experimental.pallas import tpu as pltpu
from jax.sharding import PartitionSpec as P

HD = 128
MESH = pl.DeviceIdType.MESH
VMEM_LIMIT = 56 * 1024 * 1024
ACROSS = (((1,), (1,)), ((), ()))
DOWN = (((0,), (0,)), ((), ()))


def mult(a, b, dims):
    return lax.dot_general(a, b, dims, preferred_element_type=jnp.float32)


def head_probs(query, key):
    length = query.shape[0]
    scores = mult(query, key, ACROSS) * HD ** (-0.5)
    row_ids = lax.broadcasted_iota(jnp.int32, (length, length), 0)
    col_ids = lax.broadcasted_iota(jnp.int32, (length, length), 1)
    scores = jnp.where(row_ids >= col_ids, scores, -jnp.inf)
    top = jnp.max(scores, axis=-1, keepdims=True)
    raised = jnp.exp(scores - top)
    return raised / jnp.sum(raised, axis=-1, keepdims=True)


def tick(
    sections,
    group,
    slot_ref,
    residual_ref,
    weight_ref,
    attn_ref,
    stash_ref,
    grad_ref,
    fwd_ref,
    qkv_ref,
    evict_ref,
    weight,
    attn,
    stash,
    grad,
    resid,
    request,
    stored,
    context,
    grad_context,
    own_sum,
    sums_out,
    sums_in,
    piece_out,
    piece_in,
    qkv,
    local_sem,
    evict_send,
    evict_recv,
    request_send,
    request_recv,
    sums_send,
    sums_recv,
    piece_send,
    piece_recv,
    gather_send,
    gather_recv,
):
    section = lax.axis_index("pipe")
    shard = lax.axis_index("tensor")
    partner = lax.rem(section + sections // 2, sections)
    following = lax.rem(section + 1, sections)
    before = lax.rem(section + sections - 1, sections)
    parts, rows, local = attn.shape
    width = piece_out.shape[1]
    heads = local // HD

    def peer(distance):
        return lax.rem(shard + distance, group)

    def lanes(index, size):
        return pl.ds(pl.multiple_of(index * size, size), size)

    loads = []
    for number, (source, target) in enumerate(
        (
            (stash_ref.at[0], stash),
            (attn_ref.at[0], attn),
            (weight_ref.at[0], weight),
            (grad_ref.at[0], grad),
            (residual_ref.at[0, :, lanes(shard, width)], resid),
        )
    ):
        load = pltpu.make_async_copy(source, target, local_sem.at[number])
        load.start()
        loads.append(load)

    barrier = pltpu.get_barrier_semaphore()
    for other in (partner, following, before):
        pl.semaphore_signal(barrier, inc=1, device_id=(other, shard), device_id_type=MESH)
    for distance in range(1, group):
        pl.semaphore_signal(
            barrier, inc=1, device_id=(section, peer(distance)), device_id_type=MESH
        )
    pl.semaphore_wait(barrier, 3 + group - 1)

    evictions = [
        pltpu.make_async_remote_copy(
            src_ref=attn_ref.at[0, part],
            dst_ref=evict_ref.at[0, part],
            send_sem=evict_send.at[part],
            recv_sem=evict_recv.at[part],
            device_id=(partner, shard),
            device_id_type=MESH,
        )
        for part in range(parts)
    ]
    requests = [
        pltpu.make_async_remote_copy(
            src_ref=request.at[part],
            dst_ref=stored.at[part],
            send_sem=request_send.at[part],
            recv_sem=request_recv.at[part],
            device_id=(partner, shard),
            device_id_type=MESH,
        )
        for part in range(parts)
    ]

    evictions[0].start()
    wanted = slot_ref[partner]
    loads[0].wait()
    for part in range(parts):
        request[part] = stash[wanted, part]
        requests[part].start()

    loads[1].wait()

    def attend(head, _):
        cols = lanes(head, HD)
        probs = head_probs(attn[0, :, cols], attn[1, :, cols]).astype(jnp.bfloat16)
        values = attn[2, :, cols]
        context[:, cols] = jnp.dot(
            probs, values, preferred_element_type=jnp.float32
        ).astype(jnp.bfloat16)
        return 0

    lax.fori_loop(0, heads, attend, 0, unroll=2)

    loads[2].wait()
    transfers = []
    for distance in range(1, group):
        target = peer(distance)
        sums_out[distance - 1] = jnp.dot(
            context[...], weight[:, lanes(target, width)], preferred_element_type=jnp.float32
        )
        transfer = pltpu.make_async_remote_copy(
            src_ref=sums_out.at[distance - 1],
            dst_ref=sums_in.at[distance - 1],
            send_sem=sums_send.at[distance - 1],
            recv_sem=sums_recv.at[distance - 1],
            device_id=(section, target),
            device_id_type=MESH,
        )
        transfer.start()
        transfers.append(transfer)
    loads[4].wait()
    own_sum[...] = resid[...].astype(jnp.float32) + jnp.dot(
        context[...], weight[:, lanes(shard, width)], preferred_element_type=jnp.float32
    )

    loads[3].wait()
    tile = min(local, 2 * HD)

    def back_project(step, _):
        cols = lanes(step, tile)
        grad_context[:, cols] = mult(grad[...], weight[cols, :], ACROSS).astype(jnp.bfloat16)
        return 0

    lax.fori_loop(0, local // tile, back_project, 0)

    for transfer in transfers:
        transfer.wait()
    total = own_sum[...]
    for distance in range(1, group):
        total = total + sums_in[distance - 1]
    piece_out[...] = total.astype(jnp.bfloat16)
    hand_over = pltpu.make_async_remote_copy(
        src_ref=piece_out,
        dst_ref=piece_in,
        send_sem=piece_send.at[0],
        recv_sem=piece_recv.at[0],
        device_id=(following, shard),
        device_id_type=MESH,
    )
    hand_over.start()
    for part in range(1, parts):
        evictions[part].start()

    hand_over.wait()
    own_columns = lanes(shard, width)
    gathers = []
    for distance in range(1, group):
        gather = pltpu.make_async_remote_copy(
            src_ref=piece_in,
            dst_ref=fwd_ref.at[0, :, own_columns],
            send_sem=gather_send.at[distance - 1],
            recv_sem=gather_recv.at[distance - 1],
            device_id=(section, peer(distance)),
            device_id_type=MESH,
        )
        gather.start()
        gathers.append(gather)
    keep = pltpu.make_async_copy(piece_in, fwd_ref.at[0, :, own_columns], local_sem.at[5])
    keep.start()

    for copy in requests:
        copy.wait()

    def attend_back(head, _):
        cols = lanes(head, HD)
        query, key, value = (stored[part, :, cols] for part in range(3))
        grads = grad_context[:, cols]
        probs = head_probs(query, key)
        grad_probs = mult(grads, value, ACROSS)
        row_delta = jnp.sum(probs * grad_probs, axis=-1, keepdims=True)
        grad_scores = (probs * (grad_probs - row_delta)).astype(jnp.bfloat16)
        probs_low = probs.astype(jnp.bfloat16)
        grad_query = jnp.dot(grad_scores, key, preferred_element_type=jnp.float32)
        grad_key = mult(grad_scores, query, DOWN)
        qkv[0, :, cols] = (grad_query * HD ** (-0.5)).astype(jnp.bfloat16)
        qkv[1, :, cols] = (grad_key * HD ** (-0.5)).astype(jnp.bfloat16)
        qkv[2, :, cols] = mult(probs_low, grads, DOWN).astype(jnp.bfloat16)
        return 0

    lax.fori_loop(0, heads, attend_back, 0, unroll=2)
    put = pltpu.make_async_copy(qkv, qkv_ref.at[0], local_sem.at[6])
    put.start()

    keep.wait()
    put.wait()
    for copy in gathers:
        copy.wait()
    for copy in evictions:
        copy.wait()


def settle(*refs):
    count = (len(refs) - 2) // 3
    sources, targets, staged = (refs[start * count : (start + 1) * count] for start in range(3))
    sem_in, sem_out = refs[-2:]
    loads, stores = [], []
    for source, target, stage in zip(sources, targets, staged):
        for part in range(stage.shape[0]):
            number = len(loads)
            size = stage.shape[1]
            window = (0, pl.ds(part * size, size)) if len(source.shape) == 3 else (0, part)
            here, there = source.at[window], target.at[window]
            load = pltpu.make_async_copy(here, stage.at[part], sem_in.at[number])
            load.start()
            loads.append(load)
            stores.append(pltpu.make_async_copy(stage.at[part], there, sem_out.at[number]))
    for load, store in zip(loads, stores):
        load.wait()
        store.start()
    for store in stores:
        store.wait()


def on_device(residual, out_proj, attn_in, stash_slots, grad_in, stash_slot):
    sections = lax.axis_size("pipe")
    group = lax.axis_size("tensor")
    _, parts, rows, local = attn_in.shape
    slots = stash_slots.shape[1]
    depth = residual.shape[2]
    width = depth // group
    anywhere = pl.BlockSpec(memory_space=pl.ANY)
    results = (
        jax.ShapeDtypeStruct((1, rows, depth), jnp.bfloat16),
        jax.ShapeDtypeStruct((1, parts, rows, local), jnp.bfloat16),
        jax.ShapeDtypeStruct((1, parts, rows, local), jnp.bfloat16),
    )
    low, full = jnp.bfloat16, jnp.float32
    flops = 4 * rows * local * depth + 16 * rows * rows * local
    made = pl.pallas_call(
        functools.partial(tick, sections, group),
        out_shape=results,
        in_specs=[pl.BlockSpec(memory_space=pltpu.SMEM)] + [anywhere] * 5,
        out_specs=(anywhere,) * 3,
        scratch_shapes=[
            pltpu.VMEM((local, depth), low),
            pltpu.VMEM((parts, rows, local), low),
            pltpu.VMEM((slots, parts, rows, local), low),
            pltpu.VMEM((rows, depth), low),
            pltpu.VMEM((rows, width), low),
            pltpu.VMEM((parts, rows, local), low),
            pltpu.VMEM((parts, rows, local), low),
            pltpu.VMEM((rows, local), low),
            pltpu.VMEM((rows, local), low),
            pltpu.VMEM((rows, width), full),
            pltpu.VMEM((group - 1, rows, width), full),
            pltpu.VMEM((group - 1, rows, width), full),
            pltpu.VMEM((rows, width), low),
            pltpu.VMEM((rows, width), low),
            pltpu.VMEM((parts, rows, local), low),
            pltpu.SemaphoreType.DMA((7,)),
            pltpu.SemaphoreType.DMA((parts,)),
            pltpu.SemaphoreType.DMA((parts,)),
            pltpu.SemaphoreType.DMA((parts,)),
            pltpu.SemaphoreType.DMA((parts,)),
            pltpu.SemaphoreType.DMA((group - 1,)),
            pltpu.SemaphoreType.DMA((group - 1,)),
            pltpu.SemaphoreType.DMA((1,)),
            pltpu.SemaphoreType.DMA((1,)),
            pltpu.SemaphoreType.DMA((group - 1,)),
            pltpu.SemaphoreType.DMA((group - 1,)),
        ],
        compiler_params=pltpu.CompilerParams(
            collective_id=0, has_side_effects=True, vmem_limit_bytes=VMEM_LIMIT
        ),
        cost_estimate=pl.CostEstimate(
            flops=flops, bytes_accessed=2 * local * depth, transcendentals=2 * rows * local
        ),
        name="tick",
    )(stash_slot, residual, out_proj, attn_in, stash_slots, grad_in)
    bands = 4
    return pl.pallas_call(
        settle,
        out_shape=results,
        in_specs=[anywhere] * 3,
        out_specs=(anywhere,) * 3,
        scratch_shapes=[
            pltpu.VMEM((bands, rows // bands, depth), low),
            pltpu.VMEM((parts, rows, local), low),
            pltpu.VMEM((parts, rows, local), low),
            pltpu.SemaphoreType.DMA((bands + 2 * parts,)),
            pltpu.SemaphoreType.DMA((bands + 2 * parts,)),
        ],
        compiler_params=pltpu.CompilerParams(vmem_limit_bytes=VMEM_LIMIT),
        name="settle",
    )(*made)


def solution(mesh):
    in_specs = (
        P("pipe", None, None),
        P("pipe", "tensor", None),
        P("pipe", None, None, "tensor"),
        P("pipe", None, None, None, "tensor"),
        P("pipe", None, None),
        P(),
    )
    out_specs = (
        P("pipe", None, None),
        P("pipe", None, None, "tensor"),
        P("pipe", None, None, "tensor"),
    )
    return jax.shard_map(
        on_device, mesh=mesh, in_specs=in_specs, out_specs=out_specs, check_vma=False
    )
```

```python
import functools

import jax
import jax.numpy as jnp
from jax import lax
from jax.experimental import pallas as pl
from jax.experimental.pallas import tpu as pltpu
from jax.sharding import PartitionSpec as P

HD = 128
MESH = pl.DeviceIdType.MESH
VMEM_LIMIT = 56 * 1024 * 1024
ACROSS = (((1,), (1,)), ((), ()))
DOWN = (((0,), (0,)), ((), ()))


def mult(a, b, dims):
    return lax.dot_general(a, b, dims, preferred_element_type=jnp.float32)


def head_probs(query, key):
    length = query.shape[0]
    scores = mult(query, key, ACROSS) * HD ** (-0.5)
    row_ids = lax.broadcasted_iota(jnp.int32, (length, length), 0)
    col_ids = lax.broadcasted_iota(jnp.int32, (length, length), 1)
    scores = jnp.where(row_ids >= col_ids, scores, -jnp.inf)
    top = jnp.max(scores, axis=-1, keepdims=True)
    raised = jnp.exp(scores - top)
    return raised / jnp.sum(raised, axis=-1, keepdims=True)


def tick(
    sections,
    group,
    slot_ref,
    residual_ref,
    weight_ref,
    attn_ref,
    stash_ref,
    grad_ref,
    fwd_ref,
    qkv_ref,
    evict_ref,
    weight,
    attn,
    stash,
    grad,
    resid,
    request,
    stored,
    context,
    grad_context,
    own_sum,
    mate_out,
    mate_in,
    cross_in,
    piece_out,
    piece_in,
    relayed,
    qkv,
    local_sem,
    evict_send,
    evict_recv,
    request_send,
    request_recv,
    mate_send,
    mate_recv,
    cross_send,
    cross_recv,
    piece_send,
    piece_recv,
    relay_send,
    relay_recv,
    gather_send,
    gather_recv,
    pass_send,
    pass_recv,
):
    section = lax.axis_index("pipe")
    shard = lax.axis_index("tensor")
    partner = lax.rem(section + sections // 2, sections)
    following = lax.rem(section + 1, sections)
    before = lax.rem(section + sections - 1, sections)
    two_on = lax.rem(section + 2, sections)
    two_back = lax.rem(section + sections - 2, sections)
    odd = lax.rem(section, 2) == 1
    chips = group // 2
    chip, core = shard // 2, lax.rem(shard, 2)
    mate = shard + 1 - 2 * core
    parts, rows, local = attn.shape
    width = piece_out.shape[1]
    heads = local // HD

    def on_chip(distance, which):
        return lax.rem(chip + distance, chips) * 2 + which

    def lanes(index, size):
        return pl.ds(pl.multiple_of(index * size, size), size)

    loads = []
    for number, (source, target) in enumerate(
        (
            (stash_ref.at[0], stash),
            (attn_ref.at[0], attn),
            (weight_ref.at[0], weight),
            (grad_ref.at[0], grad),
            (residual_ref.at[0, :, lanes(shard, width)], resid),
        )
    ):
        load = pltpu.make_async_copy(source, target, local_sem.at[number])
        load.start()
        loads.append(load)

    barrier = pltpu.get_barrier_semaphore()
    for other in (partner, following, before, two_on, two_back):
        pl.semaphore_signal(barrier, inc=1, device_id=(other, shard), device_id_type=MESH)
    for other in [mate] + [on_chip(distance, core) for distance in range(1, chips)]:
        pl.semaphore_signal(barrier, inc=1, device_id=(section, other), device_id_type=MESH)
    pl.semaphore_wait(barrier, 5 + chips)

    def remote(source, target, send, recv, number, where):
        return pltpu.make_async_remote_copy(
            src_ref=source,
            dst_ref=target,
            send_sem=send.at[number],
            recv_sem=recv.at[number],
            device_id=where,
            device_id_type=MESH,
        )

    evictions = [
        remote(
            attn_ref.at[0, part], evict_ref.at[0, part], evict_send, evict_recv, part, (partner, shard)
        )
        for part in range(parts)
    ]
    requests = [
        remote(
            request.at[part], stored.at[part], request_send, request_recv, part, (partner, shard)
        )
        for part in range(parts)
    ]

    evictions[0].start()
    wanted = slot_ref[partner]
    loads[0].wait()
    for part in range(parts):
        request[part] = stash[wanted, part]
        if part < parts - 1:
            requests[part].start()

    loads[1].wait()

    def attend(head, _):
        cols = lanes(head, HD)
        probs = head_probs(attn[0, :, cols], attn[1, :, cols]).astype(jnp.bfloat16)
        values = attn[2, :, cols]
        context[:, cols] = jnp.dot(
            probs, values, preferred_element_type=jnp.float32
        ).astype(jnp.bfloat16)
        return 0

    lax.fori_loop(0, heads, attend, 0, unroll=2)

    loads[2].wait()

    def branch(piece):
        return jnp.dot(
            context[...], weight[:, lanes(piece, width)], preferred_element_type=jnp.float32
        )

    order = list(range(1, chips)) + [0]
    mates, crossings = {}, {}

    def give_mate(distance):
        mate_out[distance] = branch(on_chip(distance, 1 - core))
        mates[distance] = remote(
            mate_out.at[distance],
            mate_in.at[distance],
            mate_send,
            mate_recv,
            distance,
            (section, mate),
        )
        mates[distance].start()

    for distance in order[:-1]:
        give_mate(distance)
    for distance in order[:-1]:
        own_sum[distance] = branch(on_chip(distance, core))
    give_mate(0)
    for distance in order[:-1]:
        mates[distance].wait_recv()
        own_sum[distance] = own_sum[distance] + mate_in[distance]
        crossings[distance] = remote(
            own_sum.at[distance],
            cross_in.at[distance - 1],
            cross_send,
            cross_recv,
            distance - 1,
            (section, on_chip(distance, core)),
        )
        crossings[distance].start()
    loads[4].wait()
    own_sum[0] = resid[...].astype(jnp.float32) + branch(shard)

    loads[3].wait()
    tile = min(local, 2 * HD)

    def back_project(step, _):
        cols = lanes(step, tile)
        grad_context[:, cols] = mult(grad[...], weight[cols, :], ACROSS).astype(jnp.bfloat16)
        return 0

    lax.fori_loop(0, local // tile, back_project, 0)

    mates[0].wait_recv()
    total = own_sum[0] + mate_in[0]
    for distance in range(1, chips):
        crossings[distance].wait_recv()
        total = total + cross_in[distance - 1]
    piece_out[...] = total.astype(jnp.bfloat16)

    half = rows // 2
    upper, lower = pl.ds(0, half), pl.ds(half, half)
    direct_upper = remote(
        piece_out.at[upper], piece_in.at[upper], piece_send, piece_recv, 0, (following, shard)
    )
    direct_lower = remote(
        piece_out.at[lower], piece_in.at[lower], piece_send, piece_recv, 1, (following, shard)
    )
    detour = remote(
        piece_out.at[lower], relayed, relay_send, relay_recv, 0, (before, shard)
    )
    onward = remote(
        relayed, piece_in.at[lower], relay_send, piece_recv, 1, (two_on, shard)
    )
    direct_upper.start()

    @pl.when(odd)
    def _():
        detour.start()

    @pl.when(jnp.logical_not(odd))
    def _():
        direct_lower.start()
        detour.wait_recv()
        onward.start()

    requests[parts - 1].start()
    for part in range(1, parts):
        evictions[part].start()

    direct_upper.wait_recv()
    direct_lower.wait_recv()
    own_columns = lanes(shard, width)
    keep = pltpu.make_async_copy(piece_in, fwd_ref.at[0, :, own_columns], local_sem.at[5])
    keep.start()
    gathers, passes = [], []
    for distance in list(range(1, chips)) + [0]:
        target = mate if distance == 0 else on_chip(distance, core)
        gather = remote(
            piece_in,
            fwd_ref.at[0, :, own_columns],
            gather_send,
            gather_recv,
            distance,
            (section, target),
        )
        gather.start()
        gathers.append(gather)
    for distance in range(1, chips):
        gathers[distance - 1].wait_recv()
        columns = lanes(on_chip(chips - distance, core), width)
        arrived = fwd_ref.at[0, :, columns]
        passed = remote(arrived, arrived, pass_send, pass_recv, distance - 1, (section, mate))
        passed.start()
        passes.append(passed)

    for copy in requests:
        copy.wait()

    def attend_back(head, _):
        cols = lanes(head, HD)
        query, key, value = (stored[part, :, cols] for part in range(3))
        grads = grad_context[:, cols]
        probs = head_probs(query, key)
        grad_probs = mult(grads, value, ACROSS)
        row_delta = jnp.sum(probs * grad_probs, axis=-1, keepdims=True)
        grad_scores = (probs * (grad_probs - row_delta)).astype(jnp.bfloat16)
        probs_low = probs.astype(jnp.bfloat16)
        grad_query = jnp.dot(grad_scores, key, preferred_element_type=jnp.float32)
        grad_key = mult(grad_scores, query, DOWN)
        qkv[0, :, cols] = (grad_query * HD ** (-0.5)).astype(jnp.bfloat16)
        qkv[1, :, cols] = (grad_key * HD ** (-0.5)).astype(jnp.bfloat16)
        qkv[2, :, cols] = mult(probs_low, grads, DOWN).astype(jnp.bfloat16)
        return 0

    lax.fori_loop(0, heads, attend_back, 0, unroll=2)
    put = pltpu.make_async_copy(qkv, qkv_ref.at[0], local_sem.at[6])
    put.start()

    keep.wait()
    put.wait()
    for copy in list(mates.values()) + list(crossings.values()) + gathers:
        copy.wait_send()
    direct_upper.wait_send()

    @pl.when(odd)
    def _():
        detour.wait_send()

    @pl.when(jnp.logical_not(odd))
    def _():
        direct_lower.wait_send()
        onward.wait_send()

    gathers[-1].wait_recv()
    for copy in passes + evictions:
        copy.wait()


def settle(*refs):
    count = (len(refs) - 2) // 3
    sources, targets, staged = (refs[start * count : (start + 1) * count] for start in range(3))
    sem_in, sem_out = refs[-2:]
    loads, stores = [], []
    for source, target, stage in zip(sources, targets, staged):
        for part in range(stage.shape[0]):
            number = len(loads)
            size = stage.shape[1]
            window = (0, pl.ds(part * size, size)) if len(source.shape) == 3 else (0, part)
            here, there = source.at[window], target.at[window]
            load = pltpu.make_async_copy(here, stage.at[part], sem_in.at[number])
            load.start()
            loads.append(load)
            stores.append(pltpu.make_async_copy(stage.at[part], there, sem_out.at[number]))
    for load, store in zip(loads, stores):
        load.wait()
        store.start()
    for store in stores:
        store.wait()


def on_device(residual, out_proj, attn_in, stash_slots, grad_in, stash_slot):
    sections = lax.axis_size("pipe")
    group = lax.axis_size("tensor")
    _, parts, rows, local = attn_in.shape
    slots = stash_slots.shape[1]
    depth = residual.shape[2]
    width = depth // group
    chips = group // 2
    anywhere = pl.BlockSpec(memory_space=pl.ANY)
    results = (
        jax.ShapeDtypeStruct((1, rows, depth), jnp.bfloat16),
        jax.ShapeDtypeStruct((1, parts, rows, local), jnp.bfloat16),
        jax.ShapeDtypeStruct((1, parts, rows, local), jnp.bfloat16),
    )
    low, full = jnp.bfloat16, jnp.float32
    flops = 4 * rows * local * depth + 16 * rows * rows * local
    made = pl.pallas_call(
        functools.partial(tick, sections, group),
        out_shape=results,
        in_specs=[pl.BlockSpec(memory_space=pltpu.SMEM)] + [anywhere] * 5,
        out_specs=(anywhere,) * 3,
        scratch_shapes=[
            pltpu.VMEM((local, depth), low),
            pltpu.VMEM((parts, rows, local), low),
            pltpu.VMEM((slots, parts, rows, local), low),
            pltpu.VMEM((rows, depth), low),
            pltpu.VMEM((rows, width), low),
            pltpu.VMEM((parts, rows, local), low),
            pltpu.VMEM((parts, rows, local), low),
            pltpu.VMEM((rows, local), low),
            pltpu.VMEM((rows, local), low),
            pltpu.VMEM((chips, rows, width), full),
            pltpu.VMEM((chips, rows, width), full),
            pltpu.VMEM((chips, rows, width), full),
            pltpu.VMEM((chips - 1, rows, width), full),
            pltpu.VMEM((rows, width), low),
            pltpu.VMEM((rows, width), low),
            pltpu.VMEM((rows // 2, width), low),
            pltpu.VMEM((parts, rows, local), low),
            pltpu.SemaphoreType.DMA((7,)),
            pltpu.SemaphoreType.DMA((parts,)),
            pltpu.SemaphoreType.DMA((parts,)),
            pltpu.SemaphoreType.DMA((parts,)),
            pltpu.SemaphoreType.DMA((parts,)),
            pltpu.SemaphoreType.DMA((chips,)),
            pltpu.SemaphoreType.DMA((chips,)),
            pltpu.SemaphoreType.DMA((chips - 1,)),
            pltpu.SemaphoreType.DMA((chips - 1,)),
            pltpu.SemaphoreType.DMA((2,)),
            pltpu.SemaphoreType.DMA((2,)),
            pltpu.SemaphoreType.DMA((2,)),
            pltpu.SemaphoreType.DMA((1,)),
            pltpu.SemaphoreType.DMA((chips,)),
            pltpu.SemaphoreType.DMA((chips,)),
            pltpu.SemaphoreType.DMA((chips - 1,)),
            pltpu.SemaphoreType.DMA((chips - 1,)),
        ],
        compiler_params=pltpu.CompilerParams(
            collective_id=0, has_side_effects=True, vmem_limit_bytes=VMEM_LIMIT
        ),
        cost_estimate=pl.CostEstimate(
            flops=flops, bytes_accessed=2 * local * depth, transcendentals=2 * rows * local
        ),
        name="tick",
    )(stash_slot, residual, out_proj, attn_in, stash_slots, grad_in)
    bands = 4
    return pl.pallas_call(
        settle,
        out_shape=results,
        in_specs=[anywhere] * 3,
        out_specs=(anywhere,) * 3,
        scratch_shapes=[
            pltpu.VMEM((bands, rows // bands, depth), low),
            pltpu.VMEM((parts, rows, local), low),
            pltpu.VMEM((parts, rows, local), low),
            pltpu.SemaphoreType.DMA((bands + 2 * parts,)),
            pltpu.SemaphoreType.DMA((bands + 2 * parts,)),
        ],
        compiler_params=pltpu.CompilerParams(vmem_limit_bytes=VMEM_LIMIT),
        name="settle",
    )(*made)


def solution(mesh):
    in_specs = (
        P("pipe", None, None),
        P("pipe", "tensor", None),
        P("pipe", None, None, "tensor"),
        P("pipe", None, None, None, "tensor"),
        P("pipe", None, None),
        P(),
    )
    out_specs = (
        P("pipe", None, None),
        P("pipe", None, None, "tensor"),
        P("pipe", None, None, "tensor"),
    )
    return jax.shard_map(
        on_device, mesh=mesh, in_specs=in_specs, out_specs=out_specs, check_vma=False
    )
```
